128 devices in a mesh: depth: 4 (over y_hi, core), row: 4 (over x), col: 8 (over z, y_lo).
Axes of the slice: x: 4, y: 4 (y_hi: 2, y_lo: 2; y = y_hi * 2 + y_lo), z: 4, core: 2. Of those that a mesh axis runs over, the one named last changes fastest.
Arguments:
- inputs: bfloat16 [1024, 6144], P(('depth', 'col'), 'row'), may hold values from -6 to 6
- in_weight: bfloat16 [6144, 24576], P(('row', 'depth'), 'col'), may hold values from -0.078125 to 0.078125
- out_weight: bfloat16 [24576, 6144], P(('col', 'depth'), 'row'), may hold values from -0.0390625 to 0.0390625
- out_grad: bfloat16 [1024, 6144], P(('depth', 'col'), 'row'), may hold values from -6 to 6
Outputs:
- mixed: bfloat16 [1024, 6144], P(('depth', 'col'), 'row')
- grad_in: bfloat16 [1024, 6144], P(('depth', 'col'), 'row')
- grad_w_in: bfloat16 [6144, 24576], P(('row', 'depth'), 'col')
- grad_w_out: bfloat16 [24576, 6144], P(('col', 'depth'), 'row')
The draws below stay inside these ranges and needn't reach their ends.
All inputs are finite; a program needn't handle non-finite values.
Results may differ from the reference program's by a relative error of at most 0.025.
Values may be sent and summed in bfloat16 or wider, within the bound.
No kernel may reach another device: no remote copies, remote signals or barrier semaphores. Data moves between devices by JAX's collectives and lax.ppermute only.
A program may use at most 128 MiB of HBM per device.

```python
import math
import jax
import jax.numpy as jnp
from jax import lax

FEATS = 6144
UNITS = 24576
TOK_GRP = 256
TOKENS = 1024
N_DEPTH = 4
N_ROW = 4


def levels(rng, extent, cuts, least, top_value):
    def one(dim, parts):
        heights = jax.random.uniform(jax.random.fold_in(jax.random.fold_in(rng, 6), dim), (parts,), jnp.float32, least / len(cuts), top_value / len(cuts))
        return jnp.repeat(jnp.exp(heights), extent[dim] // parts).reshape((-1,) + (1,) * (len(extent) - dim - 1))

    factor_of = one(*cuts[0])
    for cut in cuts[1:]:
        factor_of = factor_of * one(*cut)
    return factor_of


def noise(key, extent, scale, limit, shards=(), dtype=jnp.bfloat16):
    array = scale * jax.random.normal(key, extent, jnp.float32)
    if shards:
        array = array * levels(key, extent, shards, -0.22, 0.18)
    return jnp.clip(array, -limit, limit).astype(dtype)


def setup_inputs(seed: int = 0) -> dict:
    arg_keys = jax.random.split(jax.random.key(seed), 5)
    inputs = noise(arg_keys[0], (TOKENS, FEATS), 1.0, 6.0, ((0, 32), (1, 4)))
    in_weight = noise(arg_keys[1], (FEATS, UNITS), FEATS ** -0.5, 0.078125, ((0, 16), (1, 8)))
    out_weight = noise(arg_keys[2], (UNITS, FEATS), UNITS ** -0.5, 0.0390625, ((0, 32), (1, 4)))
    out_grad = noise(arg_keys[3], (TOKENS, FEATS), 1.0, 6.0, ((0, 32), (1, 4)))
    return dict(inputs=inputs, in_weight=in_weight, out_weight=out_weight, out_grad=out_grad)


GELU_SCALE = math.sqrt(2.0 / math.pi)
CUBIC = 0.044715

def gelu_value(value):
    inner = GELU_SCALE * (value + CUBIC * value * value * value)
    return 0.5 * value * (1.0 + jnp.tanh(inner))

def gelu_slope(value):
    inner = GELU_SCALE * (value + CUBIC * value * value * value)
    tanh_value = jnp.tanh(inner)
    return 0.5 * (1.0 + tanh_value) + 0.5 * value * (1.0 - tanh_value * tanh_value) * GELU_SCALE * (1.0 + 3.0 * CUBIC * value * value)

def rounded(term):
    return lax.optimization_barrier(term.astype(jnp.bfloat16)).astype(jnp.float32)

def reference(inputs, in_weight, out_weight, out_grad):
    block = FEATS // N_ROW
    preact = jnp.zeros((TOKENS, UNITS), jnp.float32)
    grad_act = jnp.zeros((TOKENS, UNITS), jnp.float32)
    for index in range(N_ROW):
        lower = index * block
        term = jnp.dot(inputs[:, lower:lower + block], in_weight[lower:lower + block, :], preferred_element_type=jnp.float32)
        preact = preact + rounded(term)
        back = jnp.dot(out_grad[:, lower:lower + block], out_weight[:, lower:lower + block].T, preferred_element_type=jnp.float32)
        grad_act = grad_act + rounded(back)
    act_full = gelu_value(preact).astype(jnp.bfloat16)
    mixed = jnp.dot(act_full, out_weight, preferred_element_type=jnp.float32).astype(jnp.bfloat16)
    grad_pre = (grad_act * gelu_slope(preact)).astype(jnp.bfloat16)
    grad_in = jnp.dot(grad_pre, in_weight.T, preferred_element_type=jnp.float32).astype(jnp.bfloat16)
    sum_in = jnp.zeros((FEATS, UNITS), jnp.float32)
    sum_out = jnp.zeros((UNITS, FEATS), jnp.float32)
    for group in range(N_DEPTH):
        first = group * TOK_GRP
        sum_in = sum_in + rounded(jnp.dot(inputs[first:first + TOK_GRP, :].T, grad_pre[first:first + TOK_GRP, :], preferred_element_type=jnp.float32))
        sum_out = sum_out + rounded(jnp.dot(act_full[first:first + TOK_GRP, :].T, out_grad[first:first + TOK_GRP, :], preferred_element_type=jnp.float32))
    return (mixed, grad_in, sum_in.astype(jnp.bfloat16), sum_out.astype(jnp.bfloat16))
```

```python
import math

import jax
import jax.numpy as jnp
from jax import lax
from jax.sharding import Mesh, PartitionSpec as P

GELU_SCALE = math.sqrt(2.0 / math.pi)
CUBIC = 0.044715
BACK_DIMS = (((1,), (1,)), ((), ()))
LEAD_DIMS = (((0,), (0,)), ((), ()))
PLAIN_DIMS = (((1,), (0,)), ((), ()))
AXES = ("b", "c", "x", "z", "a")
BF16, F32 = jnp.bfloat16, jnp.float32


def place(x, y, z, c):
    b, a = divmod(y % 4, 2)
    return (((b * 2 + c) * 4 + x % 4) * 4 + z % 4) * 2 + a


def shift(value, dx=0, dy=0, dz=0, fc=0):
    pairs = [
        (place(x, y, z, c), place(x + dx, y + dy, z + dz, c ^ fc))
        for x in range(4)
        for y in range(4)
        for z in range(4)
        for c in range(2)
    ]
    return lax.ppermute(value, AXES, pairs)


def mul(left, right, dims):
    return lax.dot_general(left, right, dims, preferred_element_type=F32).astype(BF16)


def gelu_both(value):
    inner = GELU_SCALE * (value + CUBIC * value * value * value)
    tanh_value = jnp.tanh(inner)
    slope = 0.5 * (1.0 + tanh_value) + 0.5 * value * (1.0 - tanh_value * tanh_value) * GELU_SCALE * (
        1.0 + 3.0 * CUBIC * value * value
    )
    return 0.5 * value * (1.0 + tanh_value), slope


def at(blocks, index):
    return lax.dynamic_index_in_dim(blocks, index, 0, keepdims=False)


def put(parts):
    whole = jnp.zeros((len(parts),) + parts[0][1].shape, parts[0][1].dtype)
    for index, block in parts:
        whole = lax.dynamic_update_index_in_dim(whole, block, index, 0)
    return whole


def sum_x(part, me):
    total = at(part, me).astype(F32)
    for step in (1, 3, 2):
        total = total + shift(at(part, (me + step) % 4), dx=step).astype(F32)
    return total


def gather_x(block, me):
    return put([(me, block)] + [((me + step) % 4, shift(block, dx=-step)) for step in (1, 3, 2)])


def sum_tokens(part):
    rows = part.reshape(4, 128, part.shape[1])
    total = rows[0].astype(F32)
    for step in (1, 3, 2):
        total = total + shift(rows[step], dz=step).astype(F32)
    rows = total.astype(BF16).reshape(4, 32, part.shape[1])
    total = rows[0].astype(F32)
    for step in (1, 3, 2):
        total = total + shift(rows[step], dy=step).astype(F32)
    return total.astype(BF16)


def body(inputs, in_weight, out_weight, out_grad):
    b, c, x = lax.axis_index("b"), lax.axis_index("c"), lax.axis_index("x")
    units = 1536

    both = jnp.stack([out_grad, inputs])
    got = [both] + [shift(both, dy=-step) for step in (1, 2, 3)]
    grad_128 = jnp.concatenate([v[0] for v in got])
    tok_128 = jnp.concatenate([v[1] for v in got])
    grad_rows = jnp.concatenate([grad_128] + [shift(grad_128, dz=-step) for step in (1, 2, 3)])
    tok_rows = jnp.concatenate([tok_128] + [shift(tok_128, dz=-step) for step in (1, 2, 3)])

    out_tile = put([(c, out_weight), (1 - c, shift(out_weight, fc=1))]).reshape(2 * 768, 1536)
    own = lax.dynamic_slice(in_weight, (0, b * units), (384, units))
    away = shift(lax.dynamic_slice(in_weight, (0, (1 - b) * units), (384, units)), dy=2)
    in_tile = put(
        [
            (2 * b + c, own),
            (2 * (1 - b) + c, away),
            (2 * b + 1 - c, shift(own, fc=1)),
            (2 * (1 - b) + 1 - c, shift(away, fc=1)),
        ]
    ).reshape(1536, units)

    grad_part = mul(grad_rows, out_tile, BACK_DIMS).reshape(4, 128, units)
    grad_act = sum_x(grad_part, x)
    pre_part = mul(tok_rows, in_tile, PLAIN_DIMS).reshape(4, 128, units)
    preact = sum_x(pre_part, x)
    act, slope = gelu_both(preact)
    grad_pre = gather_x((grad_act * slope).astype(BF16), x).reshape(512, units)
    act = gather_x(act.astype(BF16), x).reshape(512, units)

    term = mul(tok_rows, grad_pre, LEAD_DIMS).reshape(2, 2, 384, units)
    mine = lax.dynamic_index_in_dim(term, c, 1, keepdims=False)
    other = lax.dynamic_index_in_dim(term, 1 - c, 1, keepdims=False)
    rows = (mine.astype(F32) + shift(other, fc=1).astype(F32)).astype(BF16)
    grad_w_in = put([(b, at(rows, b)), (1 - b, shift(at(rows, 1 - b), dy=2))])
    grad_w_in = jnp.concatenate([grad_w_in[0], grad_w_in[1]], axis=1)

    grad_in = sum_tokens(mul(grad_pre, in_tile, BACK_DIMS))
    mixed = sum_tokens(mul(act, out_tile, PLAIN_DIMS))

    term = mul(act, grad_rows, LEAD_DIMS).reshape(2, 768, 1536)
    grad_w_out = (at(term, c).astype(F32) + shift(at(term, 1 - c), fc=1).astype(F32)).astype(BF16)
    return (mixed, grad_in, grad_w_in, grad_w_out)


def solution(mesh):
    fine = Mesh(mesh.devices.reshape(2, 2, 4, 4, 2), AXES)
    tokens = P(("b", "c", "z", "a"), "x")
    w_in = P(("x", "b", "c"), ("z", "a"))
    w_out = P(("z", "a", "b", "c"), "x")
    return jax.shard_map(
        body,
        mesh=fine,
        in_specs=(tokens, w_in, w_out, tokens),
        out_specs=(tokens, tokens, w_in, w_out),
        check_vma=False,
    )
```

```python
import math

import jax
import jax.numpy as jnp
from jax import lax
from jax.experimental import pallas as pl
from jax.experimental.pallas import tpu as pltpu
from jax.sharding import Mesh, PartitionSpec as P

GELU_SCALE = math.sqrt(2.0 / math.pi)
CUBIC = 0.044715
BACK_DIMS = (((1,), (1,)), ((), ()))
LEAD_DIMS = (((0,), (0,)), ((), ()))
PLAIN_DIMS = (((1,), (0,)), ((), ()))
AXES = ("b", "c", "x", "z", "a")
BF16, F32 = jnp.bfloat16, jnp.float32
ANY = pl.BlockSpec(memory_space=pl.ANY)
SMEM = pl.BlockSpec(memory_space=pltpu.SMEM)
WHOLE = pl.BlockSpec(memory_space=pltpu.VMEM)
SMALL = pl.CostEstimate(flops=1024, bytes_accessed=1024, transcendentals=0)


def place(x, y, z, c):
    b, a = divmod(y % 4, 2)
    return (((b * 2 + c) * 4 + x % 4) * 4 + z % 4) * 2 + a


def shift(value, dx=0, dy=0, dz=0, fc=0):
    pairs = [
        (place(x, y, z, c), place(x + dx, y + dy, z + dz, c ^ fc))
        for x in range(4)
        for y in range(4)
        for z in range(4)
        for c in range(2)
    ]
    return lax.ppermute(value, AXES, pairs)


def mul(left, right, dims):
    return lax.dot_general(left, right, dims, preferred_element_type=F32).astype(BF16)


def gelu_both(value):
    inner = GELU_SCALE * (value + CUBIC * value * value * value)
    tanh_value = jnp.tanh(inner)
    slope = 0.5 * (1.0 + tanh_value) + 0.5 * value * (1.0 - tanh_value * tanh_value) * GELU_SCALE * (
        1.0 + 3.0 * CUBIC * value * value
    )
    return 0.5 * value * (1.0 + tanh_value), slope


def at(blocks, index):
    return lax.dynamic_index_in_dim(blocks, index, 0, keepdims=False)


def after(value, *others):
    return lax.optimization_barrier((value,) + others)[0]


def call(kernel, name, outs, operands, specs=None, scratch=(), after=(), vmem=12, grid=(), out_specs=None):
    n, m = len(operands), len(after)

    def waiting(*refs):
        kernel(*refs[:n], *refs[n + m :])

    return pl.pallas_call(
        waiting,
        grid=grid,
        out_shape=[jax.ShapeDtypeStruct(shape, BF16) for shape in outs],
        in_specs=list(specs or [ANY] * n) + [ANY] * m,
        out_specs=out_specs or [WHOLE] * len(outs),
        scratch_shapes=list(scratch),
        compiler_params=pltpu.CompilerParams(vmem_limit_bytes=vmem * 1024 * 1024),
        cost_estimate=SMALL,
        name=name,
    )(*operands, *after)


def numbers_of(numbers):
    return jnp.stack([jnp.int32(number) for number in numbers])


def start(copies):
    for copy in copies:
        copy.start()
    return copies


def finish(copies):
    for copy in copies:
        copy.wait()


def spread(blocks, after):
    def kernel(*refs):
        outs, sems = refs[4:6], refs[6]
        finish(
            start(
                [
                    pltpu.make_async_copy(refs[i].at[pl.ds(h * 32, 32)], outs[h].at[pl.ds(i * 32, 32)], sems.at[i, h])
                    for i in range(4)
                    for h in range(2)
                ]
            )
        )

    return call(kernel, "spread", [(128, 1536)] * 2, blocks, None, [pltpu.SemaphoreType.DMA((4, 2))], after, 4)


def held(rows, after):
    def kernel(rows_ref, out_ref, sem):
        finish(start([pltpu.make_async_copy(rows_ref, out_ref, sem.at[0])]))

    return call(kernel, "held", [rows.shape], [rows], None, [pltpu.SemaphoreType.DMA((1,))], after, 4)[0]


def copied(shape, parts, after=()):
    n = len(parts)

    def kernel(numbers, *refs):
        out, sems = refs[n], refs[n + 1]
        copies = []
        for i in range(n):
            rows = refs[i].shape[0]
            col, row, out_col = (numbers[3 * i + k] for k in range(3))
            source = refs[i].at[:, pl.ds(pl.multiple_of(col * 1536, 1536), 1536)]
            target = out.at[pl.ds(pl.multiple_of(row * rows, rows), rows), pl.ds(pl.multiple_of(out_col * 1536, 1536), 1536)]
            copies.append(pltpu.make_async_copy(source, target, sems.at[i]))
        finish(start(copies))

    return call(
        kernel,
        "copied",
        [shape],
        [numbers_of([v for part in parts for v in part[1:]]), *[part[0] for part in parts]],
        [SMEM] + [ANY] * n,
        [pltpu.SemaphoreType.DMA((n,))],
        after,
        6,
    )[0]


def last(terms, after):
    def kernel(*refs):
        result = total([ref[...] for ref in refs[:4]]).astype(BF16)
        refs[4][...], refs[5][...] = result[:32], result[32:]

    return call(kernel, "last", [(32, 1536)] * 2, terms, [WHOLE] * 4, (), after, 4)


def put(parts, split=1):
    blocks = [block for _, block in parts]
    n, rows, width = len(parts), blocks[0].shape[0] // split, blocks[0].shape[1]

    def kernel(index_ref, *refs):
        outs, sems = refs[n : n + split], refs[n + split]
        copies = [
            pltpu.make_async_copy(
                refs[i].at[pl.ds(h * rows, rows)],
                outs[h].at[pl.ds(pl.multiple_of(index_ref[i] * rows, rows), rows)],
                sems.at[i, h],
            )
            for i in range(n)
            for h in range(split)
        ]
        for copy in copies:
            copy.start()
        for copy in copies:
            copy.wait()

    return pl.pallas_call(
        kernel,
        out_shape=[jax.ShapeDtypeStruct((n * rows, width), BF16)] * split,
        in_specs=[pl.BlockSpec(memory_space=pltpu.SMEM)] + [pl.BlockSpec(memory_space=pl.ANY)] * n,
        out_specs=[pl.BlockSpec(memory_space=pltpu.VMEM)] * split,
        scratch_shapes=[pltpu.SemaphoreType.DMA((n, split))],
        compiler_params=pltpu.CompilerParams(vmem_limit_bytes=10 * 1024 * 1024),
        name="put",
    )(jnp.stack([jnp.int32(index) for index, _ in parts]), *blocks)


def product(blocks, places, weight, dims, keep=False, joined=False, after=(), first=(0,) * 4):
    wide, back = 512, dims == BACK_DIMS
    n, m = len(blocks), len(after)
    n_out = 1 if joined else n
    rows = 512 // n_out

    def kernel(place_ref, *refs):
        w_ref, refs_after = refs[n], refs[n + 1 + m :]
        outs, rest = refs_after[:n_out], refs_after[n_out:]
        whole, sems = rest[0], rest[1]

        @pl.when(pl.program_id(0) == 0)
        def _():
            copies = [
                pltpu.make_async_copy(
                    refs[i].at[pl.ds(first[i], 128)],
                    whole.at[pl.ds(pl.multiple_of(place_ref[i] * 128, 128), 128)],
                    sems.at[i],
                )
                for i in range(n)
            ]
            for copy in copies:
                copy.start()
            for copy in copies:
                copy.wait()

        result = lax.dot_general(whole[...], w_ref[...], dims, preferred_element_type=F32).astype(BF16)
        for i in range(n_out):
            outs[i][...] = result[i * rows : (i + 1) * rows]

    w_block = ((wide, 1536), lambda t: (t, 0)) if back else ((1536, wide), lambda t: (0, t))
    out_shape = [jax.ShapeDtypeStruct((rows, 1536), BF16)] * n_out
    out_specs = [pl.BlockSpec((rows, wide), lambda t: (0, t))] * n_out
    scratch = [pltpu.VMEM((512, 1536), BF16), pltpu.SemaphoreType.DMA((n,))]
    if keep:
        out_shape.append(jax.ShapeDtypeStruct((512, 1536), BF16))
        out_specs.append(pl.BlockSpec((512, 1536), lambda t: (0, 0)))
        scratch = scratch[1:]
    return pl.pallas_call(
        kernel,
        grid=(1536 // wide,),
        out_shape=out_shape,
        in_specs=[pl.BlockSpec(memory_space=pltpu.SMEM)]
        + [pl.BlockSpec(memory_space=pl.ANY)] * n
        + [pl.BlockSpec(*w_block)]
        + [pl.BlockSpec(memory_space=pl.ANY)] * m,
        out_specs=out_specs,
        scratch_shapes=scratch,
        compiler_params=pltpu.CompilerParams(vmem_limit_bytes=16 * 1024 * 1024),
        cost_estimate=pl.CostEstimate(flops=2 * 512 * 1536 * 1536, bytes_accessed=8 << 20, transcendentals=0),
        name="product",
    )(jnp.stack([jnp.int32(place) for place in places]), *blocks, weight, *after)


def total(parts):
    result = parts[0].astype(F32)
    for part in parts[1:]:
        result = result + part.astype(F32)
    return result


def summed(rows, me, axis):
    blocks = rows.reshape(4, rows.shape[0] // 4, rows.shape[1])
    return total([at(blocks, me)] + [shift(at(blocks, (me + i) % 4), **{axis: i}) for i in (1, 2, 3)])


def scatter(parts, axis):
    return [parts[0]] + [shift(parts[i], **{axis: i}) for i in (1, 2, 3)]


def gather(block, axis):
    return [block] + [shift(block, **{axis: -i}) for i in (1, 2, 3)]


def body(inputs, in_weight, out_weight, out_grad):
    b, c, x, z = (lax.axis_index(name) for name in ("b", "c", "x", "z"))
    units = 1536
    quarters = (0, 128, 256, 384)
    in_z = [(x + i) % 4 for i in range(4)]
    to_x = [(z + i - x) % 4 for i in range(4)]
    to_z = [(x + i - z) % 4 for i in range(4)]

    out_other = shift(out_weight, fc=1)
    own = lax.dynamic_slice(in_weight, (0, b * units), (384, units))
    own_other = shift(own, fc=1)
    both = gather(jnp.concatenate([out_grad, inputs]), "dy")
    grad_128, tok_128 = spread(both, [out_other, own_other])
    grad_blocks = gather(grad_128, "dz")
    away = shift(after(lax.dynamic_slice(in_weight, (0, (1 - b) * units), (384, units)), grad_128), dy=2)

    (out_tile,) = put([(c, out_weight), (1 - c, out_other)])
    (grad_rows,) = put([((z + i) % 4, grad_blocks[i]) for i in range(4)])
    grad_part = mul(grad_rows, out_tile, BACK_DIMS)
    grad_act = summed(grad_part, x, "dx")

    tok_rows = lax.all_gather(held(tok_128, grad_blocks), "z", axis=0, tiled=True)
    away = after(away, grad_part)
    (in_tile,) = put(
        [
            (2 * b + c, own),
            (2 * (1 - b) + c, away),
            (2 * b + 1 - c, own_other),
            (2 * (1 - b) + 1 - c, shift(away, fc=1)),
        ]
    )
    preact = summed(mul(tok_rows, in_tile, PLAIN_DIMS), x, "dx")
    act, slope = gelu_both(preact)
    pre_blocks = gather((grad_act * slope).astype(BF16), "dx")
    act_rows = lax.all_gather(act.astype(BF16), "x", axis=0, tiled=True)

    (grad_pre,) = put(list(zip(in_z, pre_blocks)))

    def columns(which):
        return jnp.concatenate(
            [lax.dynamic_slice(tok_rows, (0, (2 * i + which) * 384), (512, 384)) for i in range(2)], axis=1
        )

    tok_mine, tok_other = columns(c), columns(1 - c)

    other = shift(mul(tok_other, grad_pre, LEAD_DIMS), fc=1)
    in_part = mul(grad_pre, in_tile, BACK_DIMS)
    other, in_part = lax.optimization_barrier((other, in_part))
    in_rows = lax.psum_scatter(in_part, "z", scatter_dimension=0, tiled=True)
    rows = total([mul(tok_mine, grad_pre, LEAD_DIMS), other]).astype(BF16).reshape(2, 384, units)
    kept, sent = at(rows, b), at(rows, 1 - b)
    arrived = shift(sent, dy=2)
    act_rows = after(act_rows, sent)
    out_rows = summed(mul(act_rows, out_tile, PLAIN_DIMS), z, "dz").astype(BF16)
    grad_w_out = lax.psum_scatter(mul(act_rows, grad_rows, LEAD_DIMS), "c", scatter_dimension=0, tiled=True)
    out_rows, arrived = lax.optimization_barrier((out_rows, arrived))
    grad_w_in = copied((384, 2 * units), [(kept, 0, 0, b), (arrived, 0, 0, 1 - b)])
    parts = [jnp.concatenate([v[i * 32 : (i + 1) * 32] for v in (out_rows, in_rows)]) for i in range(4)]
    return (*last(scatter(parts, "dy"), [grad_w_in]), grad_w_in, grad_w_out)


def solution(mesh):
    fine = Mesh(mesh.devices.reshape(2, 2, 4, 4, 2), AXES)
    tokens = P(("b", "c", "z", "a"), "x")
    w_in = P(("x", "b", "c"), ("z", "a"))
    w_out = P(("z", "a", "b", "c"), "x")
    return jax.shard_map(
        body,
        mesh=fine,
        in_specs=(tokens, w_in, w_out, tokens),
        out_specs=(tokens, tokens, w_in, w_out),
        check_vma=False,
    )
```

```python
import math

import jax
import jax.numpy as jnp
from jax import lax
from jax.experimental import pallas as pl
from jax.experimental.pallas import tpu as pltpu
from jax.sharding import Mesh, PartitionSpec as P

GELU_SCALE = math.sqrt(2.0 / math.pi)
CUBIC = 0.044715
BACK_DIMS = (((1,), (1,)), ((), ()))
LEAD_DIMS = (((0,), (0,)), ((), ()))
PLAIN_DIMS = (((1,), (0,)), ((), ()))
AXES = ("b", "c", "x", "z", "a")
BF16, F32 = jnp.bfloat16, jnp.float32
ANY = pl.BlockSpec(memory_space=pl.ANY)
SMEM = pl.BlockSpec(memory_space=pltpu.SMEM)
WHOLE = pl.BlockSpec(memory_space=pltpu.VMEM)
SMALL = pl.CostEstimate(flops=1024, bytes_accessed=1024, transcendentals=0)


def place(x, y, z, c):
    b, a = divmod(y % 4, 2)
    return (((b * 2 + c) * 4 + x % 4) * 4 + z % 4) * 2 + a


def shift(value, dx=0, dy=0, dz=0, fc=0):
    pairs = [
        (place(x, y, z, c), place(x + dx, y + dy, z + dz, c ^ fc))
        for x in range(4)
        for y in range(4)
        for z in range(4)
        for c in range(2)
    ]
    return lax.ppermute(value, AXES, pairs)


def mul(left, right, dims):
    return lax.dot_general(left, right, dims, preferred_element_type=F32).astype(BF16)


def gelu_both(value):
    inner = GELU_SCALE * (value + CUBIC * value * value * value)
    tanh_value = jnp.tanh(inner)
    slope = 0.5 * (1.0 + tanh_value) + 0.5 * value * (1.0 - tanh_value * tanh_value) * GELU_SCALE * (
        1.0 + 3.0 * CUBIC * value * value
    )
    return 0.5 * value * (1.0 + tanh_value), slope


def at(blocks, index):
    return lax.dynamic_index_in_dim(blocks, index, 0, keepdims=False)


def after(value, *others):
    return lax.optimization_barrier((value,) + others)[0]


def call(kernel, name, outs, operands, specs=None, scratch=(), after=(), vmem=12, grid=(), out_specs=None):
    n, m = len(operands), len(after)

    def waiting(*refs):
        kernel(*refs[:n], *refs[n + m :])

    return pl.pallas_call(
        waiting,
        grid=grid,
        out_shape=[jax.ShapeDtypeStruct(shape, BF16) for shape in outs],
        in_specs=list(specs or [ANY] * n) + [ANY] * m,
        out_specs=out_specs or [WHOLE] * len(outs),
        scratch_shapes=list(scratch),
        compiler_params=pltpu.CompilerParams(vmem_limit_bytes=vmem * 1024 * 1024),
        cost_estimate=SMALL,
        name=name,
    )(*operands, *after)


def numbers_of(numbers):
    return jnp.stack([jnp.int32(number) for number in numbers])


def start(copies):
    for copy in copies:
        copy.start()
    return copies


def finish(copies):
    for copy in copies:
        copy.wait()


def spread(blocks, after):
    def kernel(*refs):
        outs, sems = refs[4:6], refs[6]
        finish(
            start(
                [
                    pltpu.make_async_copy(refs[i].at[pl.ds(h * 32, 32)], outs[h].at[pl.ds(i * 32, 32)], sems.at[i, h])
                    for i in range(4)
                    for h in range(2)
                ]
            )
        )

    return call(kernel, "spread", [(128, 1536)] * 2, blocks, None, [pltpu.SemaphoreType.DMA((4, 2))], after, 4)


def held(rows, after):
    def kernel(rows_ref, out_ref, sem):
        finish(start([pltpu.make_async_copy(rows_ref, out_ref, sem.at[0])]))

    return call(kernel, "held", [rows.shape], [rows], None, [pltpu.SemaphoreType.DMA((1,))], after, 4)[0]


def copied(shape, parts, after=()):
    n = len(parts)

    def kernel(numbers, *refs):
        out, sems = refs[n], refs[n + 1]
        copies = []
        for i in range(n):
            rows = refs[i].shape[0]
            col, row, out_col = (numbers[3 * i + k] for k in range(3))
            source = refs[i].at[:, pl.ds(pl.multiple_of(col * 1536, 1536), 1536)]
            target = out.at[pl.ds(pl.multiple_of(row * rows, rows), rows), pl.ds(pl.multiple_of(out_col * 1536, 1536), 1536)]
            copies.append(pltpu.make_async_copy(source, target, sems.at[i]))
        finish(start(copies))

    return call(
        kernel,
        "copied",
        [shape],
        [numbers_of([v for part in parts for v in part[1:]]), *[part[0] for part in parts]],
        [SMEM] + [ANY] * n,
        [pltpu.SemaphoreType.DMA((n,))],
        after,
        6,
    )[0]


def last(terms, after):
    def kernel(*refs):
        result = total([ref[...] for ref in refs[:4]]).astype(BF16)
        refs[4][...], refs[5][...] = result[:32], result[32:]

    return call(kernel, "last", [(32, 1536)] * 2, terms, [WHOLE] * 4, (), after, 4)


def put(parts, split=1):
    blocks = [block for _, block in parts]
    n, rows, width = len(parts), blocks[0].shape[0] // split, blocks[0].shape[1]

    def kernel(index_ref, *refs):
        outs, sems = refs[n : n + split], refs[n + split]
        copies = [
            pltpu.make_async_copy(
                refs[i].at[pl.ds(h * rows, rows)],
                outs[h].at[pl.ds(pl.multiple_of(index_ref[i] * rows, rows), rows)],
                sems.at[i, h],
            )
            for i in range(n)
            for h in range(split)
        ]
        for copy in copies:
            copy.start()
        for copy in copies:
            copy.wait()

    return pl.pallas_call(
        kernel,
        out_shape=[jax.ShapeDtypeStruct((n * rows, width), BF16)] * split,
        in_specs=[pl.BlockSpec(memory_space=pltpu.SMEM)] + [pl.BlockSpec(memory_space=pl.ANY)] * n,
        out_specs=[pl.BlockSpec(memory_space=pltpu.VMEM)] * split,
        scratch_shapes=[pltpu.SemaphoreType.DMA((n, split))],
        compiler_params=pltpu.CompilerParams(vmem_limit_bytes=10 * 1024 * 1024),
        name="put",
    )(jnp.stack([jnp.int32(index) for index, _ in parts]), *blocks)


def product(blocks, places, weight, dims, keep=False, joined=False, after=(), first=(0,) * 4):
    wide, back = 512, dims == BACK_DIMS
    n, m = len(blocks), len(after)
    n_out = 1 if joined else n
    rows = 512 // n_out

    def kernel(place_ref, *refs):
        w_ref, refs_after = refs[n], refs[n + 1 + m :]
        outs, rest = refs_after[:n_out], refs_after[n_out:]
        whole, sems = rest[0], rest[1]

        @pl.when(pl.program_id(0) == 0)
        def _():
            copies = [
                pltpu.make_async_copy(
                    refs[i].at[pl.ds(first[i], 128)],
                    whole.at[pl.ds(pl.multiple_of(place_ref[i] * 128, 128), 128)],
                    sems.at[i],
                )
                for i in range(n)
            ]
            for copy in copies:
                copy.start()
            for copy in copies:
                copy.wait()

        result = lax.dot_general(whole[...], w_ref[...], dims, preferred_element_type=F32).astype(BF16)
        for i in range(n_out):
            outs[i][...] = result[i * rows : (i + 1) * rows]

    w_block = ((wide, 1536), lambda t: (t, 0)) if back else ((1536, wide), lambda t: (0, t))
    out_shape = [jax.ShapeDtypeStruct((rows, 1536), BF16)] * n_out
    out_specs = [pl.BlockSpec((rows, wide), lambda t: (0, t))] * n_out
    scratch = [pltpu.VMEM((512, 1536), BF16), pltpu.SemaphoreType.DMA((n,))]
    if keep:
        out_shape.append(jax.ShapeDtypeStruct((512, 1536), BF16))
        out_specs.append(pl.BlockSpec((512, 1536), lambda t: (0, 0)))
        scratch = scratch[1:]
    return pl.pallas_call(
        kernel,
        grid=(1536 // wide,),
        out_shape=out_shape,
        in_specs=[pl.BlockSpec(memory_space=pltpu.SMEM)]
        + [pl.BlockSpec(memory_space=pl.ANY)] * n
        + [pl.BlockSpec(*w_block)]
        + [pl.BlockSpec(memory_space=pl.ANY)] * m,
        out_specs=out_specs,
        scratch_shapes=scratch,
        compiler_params=pltpu.CompilerParams(vmem_limit_bytes=16 * 1024 * 1024),
        cost_estimate=pl.CostEstimate(flops=2 * 512 * 1536 * 1536, bytes_accessed=8 << 20, transcendentals=0),
        name="product",
    )(jnp.stack([jnp.int32(place) for place in places]), *blocks, weight, *after)


def total(parts):
    result = parts[0].astype(F32)
    for part in parts[1:]:
        result = result + part.astype(F32)
    return result


def summed(rows, me, axis):
    blocks = rows.reshape(4, rows.shape[0] // 4, rows.shape[1])
    return total([at(blocks, me)] + [shift(at(blocks, (me + i) % 4), **{axis: i}) for i in (1, 2, 3)])


def scatter(parts, axis):
    return [parts[0]] + [shift(parts[i], **{axis: i}) for i in (1, 2, 3)]


def gather(block, axis):
    return [block] + [shift(block, **{axis: -i}) for i in (1, 2, 3)]


def body(inputs, in_weight, out_weight, out_grad):
    b, c, x, z = (lax.axis_index(name) for name in ("b", "c", "x", "z"))
    units = 1536
    quarters = (0, 128, 256, 384)
    in_z = [(x + i) % 4 for i in range(4)]
    to_x = [(z + i - x) % 4 for i in range(4)]
    to_z = [(x + i - z) % 4 for i in range(4)]

    out_other = shift(out_weight, fc=1)
    own = lax.dynamic_slice(in_weight, (0, b * units), (384, units))
    own_other = shift(own, fc=1)
    both = gather(jnp.concatenate([out_grad, inputs]), "dy")
    grad_128, tok_128 = spread(both, [out_other])
    grad_blocks = gather(grad_128, "dz")
    away = shift(after(lax.dynamic_slice(in_weight, (0, (1 - b) * units), (384, units)), grad_128), dy=2)

    (out_tile,) = put([(c, out_weight), (1 - c, out_other)])
    grad_parts = product(grad_blocks, to_x, out_tile, BACK_DIMS)
    grad_act = total(scatter(grad_parts, "dx"))

    tok_rows = lax.all_gather(after(tok_128, *grad_blocks), "z", axis=0, tiled=True)
    away = after(away, grad_parts[0])
    (in_tile,) = put(
        [
            (2 * b + c, own),
            (2 * (1 - b) + c, away),
            (2 * b + 1 - c, own_other),
            (2 * (1 - b) + 1 - c, shift(away, fc=1)),
        ]
    )
    preact = summed(mul(tok_rows, in_tile, PLAIN_DIMS), x, "dx")
    act, slope = gelu_both(preact)
    pre_blocks = gather((grad_act * slope).astype(BF16), "dx")
    act_blocks = gather(after(act.astype(BF16), *pre_blocks), "dx")

    (grad_pre,) = put(list(zip(in_z, pre_blocks)))

    def columns(which):
        return jnp.concatenate(
            [lax.dynamic_slice(tok_rows, (0, (2 * i + which) * 384), (512, 384)) for i in range(2)], axis=1
        )

    tok_mine, tok_other = columns(c), columns(1 - c)

    other = shift(mul(tok_other, grad_pre, LEAD_DIMS), fc=1)
    in_part = mul(grad_pre, in_tile, BACK_DIMS)
    other, in_part = lax.optimization_barrier((other, in_part))
    in_rows = lax.psum_scatter(in_part, "z", scatter_dimension=0, tiled=True)
    rows = total([mul(tok_mine, grad_pre, LEAD_DIMS), other]).astype(BF16).reshape(2, 384, units)
    kept, sent = at(rows, b), at(rows, 1 - b)
    arrived = shift(sent, dy=2)
    act_blocks[0] = after(act_blocks[0], sent)
    (act_rows,) = put(list(zip(in_z, act_blocks)))
    (grad_rows,) = put([((z + i) % 4, grad_blocks[i]) for i in range(4)])
    out_rows = summed(mul(act_rows, out_tile, PLAIN_DIMS), z, "dz").astype(BF16)
    grad_w_out = lax.psum_scatter(mul(act_rows, grad_rows, LEAD_DIMS), "c", scatter_dimension=0, tiled=True)
    out_rows, arrived = lax.optimization_barrier((out_rows, arrived))
    grad_w_in = copied((384, 2 * units), [(kept, 0, 0, b), (arrived, 0, 0, 1 - b)])
    parts = [jnp.concatenate([v[i * 32 : (i + 1) * 32] for v in (out_rows, in_rows)]) for i in range(4)]
    return (*last(scatter(parts, "dy"), [grad_w_in]), grad_w_in, grad_w_out)


def solution(mesh):
    fine = Mesh(mesh.devices.reshape(2, 2, 4, 4, 2), AXES)
    tokens = P(("b", "c", "z", "a"), "x")
    w_in = P(("x", "b", "c"), ("z", "a"))
    w_out = P(("z", "a", "b", "c"), "x")
    return jax.shard_map(
        body,
        mesh=fine,
        in_specs=(tokens, w_in, w_out, tokens),
        out_specs=(tokens, tokens, w_in, w_out),
        check_vma=False,
    )
```

```python
import math

import jax
import jax.numpy as jnp
from jax import lax
from jax.experimental import pallas as pl
from jax.experimental.pallas import tpu as pltpu
from jax.sharding import Mesh, PartitionSpec as P

GELU_SCALE = math.sqrt(2.0 / math.pi)
CUBIC = 0.044715
BACK_DIMS = (((1,), (1,)), ((), ()))
LEAD_DIMS = (((0,), (0,)), ((), ()))
PLAIN_DIMS = (((1,), (0,)), ((), ()))
AXES = ("b", "c", "x", "z", "a")
BF16, F32 = jnp.bfloat16, jnp.float32
ANY = pl.BlockSpec(memory_space=pl.ANY)
SMEM = pl.BlockSpec(memory_space=pltpu.SMEM)
WHOLE = pl.BlockSpec(memory_space=pltpu.VMEM)
SMALL = pl.CostEstimate(flops=1024, bytes_accessed=1024, transcendentals=0)


def place(x, y, z, c):
    b, a = divmod(y % 4, 2)
    return (((b * 2 + c) * 4 + x % 4) * 4 + z % 4) * 2 + a


def shift(value, dx=0, dy=0, dz=0, fc=0):
    pairs = [
        (place(x, y, z, c), place(x + dx, y + dy, z + dz, c ^ fc))
        for x in range(4)
        for y in range(4)
        for z in range(4)
        for c in range(2)
    ]
    return lax.ppermute(value, AXES, pairs)


def mul(left, right, dims):
    return lax.dot_general(left, right, dims, preferred_element_type=F32).astype(BF16)


def gelu_both(value):
    inner = GELU_SCALE * (value + CUBIC * value * value * value)
    tanh_value = jnp.tanh(inner)
    slope = 0.5 * (1.0 + tanh_value) + 0.5 * value * (1.0 - tanh_value * tanh_value) * GELU_SCALE * (
        1.0 + 3.0 * CUBIC * value * value
    )
    return 0.5 * value * (1.0 + tanh_value), slope


def at(blocks, index):
    return lax.dynamic_index_in_dim(blocks, index, 0, keepdims=False)


def after(value, *others):
    return lax.optimization_barrier((value,) + others)[0]


def call(kernel, name, outs, operands, specs=None, scratch=(), after=(), vmem=12, grid=(), out_specs=None):
    n, m = len(operands), len(after)

    def waiting(*refs):
        kernel(*refs[:n], *refs[n + m :])

    return pl.pallas_call(
        waiting,
        grid=grid,
        out_shape=[jax.ShapeDtypeStruct(shape, BF16) for shape in outs],
        in_specs=list(specs or [ANY] * n) + [ANY] * m,
        out_specs=out_specs or [WHOLE] * len(outs),
        scratch_shapes=list(scratch),
        compiler_params=pltpu.CompilerParams(vmem_limit_bytes=vmem * 1024 * 1024),
        cost_estimate=SMALL,
        name=name,
    )(*operands, *after)


def numbers_of(numbers):
    return jnp.stack([jnp.int32(number) for number in numbers])


def start(copies):
    for copy in copies:
        copy.start()
    return copies


def finish(copies):
    for copy in copies:
        copy.wait()


def spread(blocks, after):
    def kernel(*refs):
        outs, sems = refs[4:6], refs[6]
        finish(
            start(
                [
                    pltpu.make_async_copy(refs[i].at[pl.ds(h * 32, 32)], outs[h].at[pl.ds(i * 32, 32)], sems.at[i, h])
                    for i in range(4)
                    for h in range(2)
                ]
            )
        )

    return call(kernel, "spread", [(128, 1536)] * 2, blocks, None, [pltpu.SemaphoreType.DMA((4, 2))], after, 4)


def held(rows, after):
    def kernel(rows_ref, out_ref, sem):
        finish(start([pltpu.make_async_copy(rows_ref, out_ref, sem.at[0])]))

    return call(kernel, "held", [rows.shape], [rows], None, [pltpu.SemaphoreType.DMA((1,))], after, 4)[0]


def copied(shape, parts, after=()):
    n = len(parts)

    def kernel(numbers, *refs):
        out, sems = refs[n], refs[n + 1]
        copies = []
        for i in range(n):
            rows = refs[i].shape[0]
            col, row, out_col = (numbers[3 * i + k] for k in range(3))
            source = refs[i].at[:, pl.ds(pl.multiple_of(col * 1536, 1536), 1536)]
            target = out.at[pl.ds(pl.multiple_of(row * rows, rows), rows), pl.ds(pl.multiple_of(out_col * 1536, 1536), 1536)]
            copies.append(pltpu.make_async_copy(source, target, sems.at[i]))
        finish(start(copies))

    return call(
        kernel,
        "copied",
        [shape],
        [numbers_of([v for part in parts for v in part[1:]]), *[part[0] for part in parts]],
        [SMEM] + [ANY] * n,
        [pltpu.SemaphoreType.DMA((n,))],
        after,
        6,
    )[0]


def last(terms, after):
    def kernel(*refs):
        result = total([ref[...] for ref in refs[:4]]).astype(BF16)
        refs[4][...], refs[5][...] = result[:32], result[32:]

    return call(kernel, "last", [(32, 1536)] * 2, terms, [WHOLE] * 4, (), after, 4)


def put(parts, split=1):
    blocks = [block for _, block in parts]
    n, rows, width = len(parts), blocks[0].shape[0] // split, blocks[0].shape[1]

    def kernel(index_ref, *refs):
        outs, sems = refs[n : n + split], refs[n + split]
        copies = [
            pltpu.make_async_copy(
                refs[i].at[pl.ds(h * rows, rows)],
                outs[h].at[pl.ds(pl.multiple_of(index_ref[i] * rows, rows), rows)],
                sems.at[i, h],
            )
            for i in range(n)
            for h in range(split)
        ]
        for copy in copies:
            copy.start()
        for copy in copies:
            copy.wait()

    return pl.pallas_call(
        kernel,
        out_shape=[jax.ShapeDtypeStruct((n * rows, width), BF16)] * split,
        in_specs=[pl.BlockSpec(memory_space=pltpu.SMEM)] + [pl.BlockSpec(memory_space=pl.ANY)] * n,
        out_specs=[pl.BlockSpec(memory_space=pltpu.VMEM)] * split,
        scratch_shapes=[pltpu.SemaphoreType.DMA((n, split))],
        compiler_params=pltpu.CompilerParams(vmem_limit_bytes=10 * 1024 * 1024),
        name="put",
    )(jnp.stack([jnp.int32(index) for index, _ in parts]), *blocks)


def product(blocks, places, weight, dims, keep=False, joined=False, after=(), first=(0,) * 4):
    wide, back = 512, dims == BACK_DIMS
    n, m = len(blocks), len(after)
    n_out = 1 if joined else n
    rows = 512 // n_out

    def kernel(place_ref, *refs):
        w_ref, refs_after = refs[n], refs[n + 1 + m :]
        outs, rest = refs_after[:n_out], refs_after[n_out:]
        whole, sems = rest[0], rest[1]

        @pl.when(pl.program_id(0) == 0)
        def _():
            copies = [
                pltpu.make_async_copy(
                    refs[i].at[pl.ds(first[i], 128)],
                    whole.at[pl.ds(pl.multiple_of(place_ref[i] * 128, 128), 128)],
                    sems.at[i],
                )
                for i in range(n)
            ]
            for copy in copies:
                copy.start()
            for copy in copies:
                copy.wait()

        result = lax.dot_general(whole[...], w_ref[...], dims, preferred_element_type=F32).astype(BF16)
        for i in range(n_out):
            outs[i][...] = result[i * rows : (i + 1) * rows]

    w_block = ((wide, 1536), lambda t: (t, 0)) if back else ((1536, wide), lambda t: (0, t))
    out_shape = [jax.ShapeDtypeStruct((rows, 1536), BF16)] * n_out
    out_specs = [pl.BlockSpec((rows, wide), lambda t: (0, t))] * n_out
    scratch = [pltpu.VMEM((512, 1536), BF16), pltpu.SemaphoreType.DMA((n,))]
    if keep:
        out_shape.append(jax.ShapeDtypeStruct((512, 1536), BF16))
        out_specs.append(pl.BlockSpec((512, 1536), lambda t: (0, 0)))
        scratch = scratch[1:]
    return pl.pallas_call(
        kernel,
        grid=(1536 // wide,),
        out_shape=out_shape,
        in_specs=[pl.BlockSpec(memory_space=pltpu.SMEM)]
        + [pl.BlockSpec(memory_space=pl.ANY)] * n
        + [pl.BlockSpec(*w_block)]
        + [pl.BlockSpec(memory_space=pl.ANY)] * m,
        out_specs=out_specs,
        scratch_shapes=scratch,
        compiler_params=pltpu.CompilerParams(vmem_limit_bytes=16 * 1024 * 1024),
        cost_estimate=pl.CostEstimate(flops=2 * 512 * 1536 * 1536, bytes_accessed=8 << 20, transcendentals=0),
        name="product",
    )(jnp.stack([jnp.int32(place) for place in places]), *blocks, weight, *after)


def total(parts):
    result = parts[0].astype(F32)
    for part in parts[1:]:
        result = result + part.astype(F32)
    return result


def terms_of(rows, me, axis):
    blocks = rows.reshape(4, rows.shape[0] // 4, rows.shape[1])
    return [at(blocks, me)] + [shift(at(blocks, (me + i) % 4), **{axis: i}) for i in (1, 2, 3)]


def summed(rows, me, axis):
    return total(terms_of(rows, me, axis))


def scatter(parts, axis):
    return [parts[0]] + [shift(parts[i], **{axis: i}) for i in (1, 2, 3)]


def gather(block, axis):
    return [block] + [shift(block, **{axis: -i}) for i in (1, 2, 3)]


def body(inputs, in_weight, out_weight, out_grad):
    b, c, x, z = (lax.axis_index(name) for name in ("b", "c", "x", "z"))
    units = 1536
    quarters = (0, 128, 256, 384)
    in_z = [(x + i) % 4 for i in range(4)]
    to_x = [(z + i - x) % 4 for i in range(4)]
    to_z = [(x + i - z) % 4 for i in range(4)]

    out_other = shift(out_weight, fc=1)
    own = lax.dynamic_slice(in_weight, (0, b * units), (384, units))
    own_other = shift(own, fc=1)
    both = gather(jnp.concatenate([out_grad, inputs]), "dy")
    grad_128, tok_128 = spread(both, [out_other])
    grad_blocks = gather(grad_128, "dz")
    away = shift(after(lax.dynamic_slice(in_weight, (0, (1 - b) * units), (384, units)), grad_128), dy=2)

    (out_tile,) = put([(c, out_weight), (1 - c, out_other)])
    *grad_parts, grad_rows = product(grad_blocks, to_x, out_tile, BACK_DIMS, True)
    grad_act = total(scatter(grad_parts, "dx"))

    tok_rows = lax.all_gather(after(tok_128, *grad_blocks), "z", axis=0, tiled=True)
    away = after(away, grad_parts[0])
    (in_tile,) = put(
        [
            (2 * b + c, own),
            (2 * (1 - b) + c, away),
            (2 * b + 1 - c, own_other),
            (2 * (1 - b) + 1 - c, shift(away, fc=1)),
        ]
    )
    preact = summed(mul(tok_rows, in_tile, PLAIN_DIMS), x, "dx")
    act, slope = gelu_both(preact)
    pre_blocks = gather((grad_act * slope).astype(BF16), "dx")
    act_blocks = gather(after(act.astype(BF16), *pre_blocks), "dx")

    (grad_pre,) = put(list(zip(in_z, pre_blocks)))

    def columns(which):
        return jnp.concatenate(
            [lax.dynamic_slice(tok_rows, (0, (2 * i + which) * 384), (512, 384)) for i in range(2)], axis=1
        )

    tok_mine, tok_other = columns(c), columns(1 - c)

    other = shift(mul(tok_other, grad_pre, LEAD_DIMS), fc=1)
    in_part = mul(grad_pre, in_tile, BACK_DIMS)
    in_rows = lax.psum_scatter(in_part, "z", scatter_dimension=0, tiled=True)
    rows = total([mul(tok_mine, grad_pre, LEAD_DIMS), other]).astype(BF16).reshape(2, 384, units)
    kept, sent = at(rows, b), at(rows, 1 - b)
    arrived = shift(sent, dy=2)
    act_blocks[0] = after(act_blocks[0], sent)
    (act_rows,) = put(list(enumerate(act_blocks)))
    out_terms = terms_of(mul(act_rows, out_tile, PLAIN_DIMS), (z - x) % 4, "dz")
    grad_w_out = lax.psum_scatter(mul(act_rows, grad_rows, LEAD_DIMS), "c", scatter_dimension=0, tiled=True)
    out_terms[1], arrived = lax.optimization_barrier((out_terms[1], arrived))
    out_rows = total(out_terms).astype(BF16)
    grad_w_in = copied((384, 2 * units), [(kept, 0, 0, b), (arrived, 0, 0, 1 - b)])
    parts = [jnp.concatenate([v[i * 32 : (i + 1) * 32] for v in (out_rows, in_rows)]) for i in range(4)]
    return (*last(scatter(parts, "dy"), [grad_w_in]), grad_w_in, grad_w_out)


def solution(mesh):
    fine = Mesh(mesh.devices.reshape(2, 2, 4, 4, 2), AXES)
    tokens = P(("b", "c", "z", "a"), "x")
    w_in = P(("x", "b", "c"), ("z", "a"))
    w_out = P(("z", "a", "b", "c"), "x")
    return jax.shard_map(
        body,
        mesh=fine,
        in_specs=(tokens, w_in, w_out, tokens),
        out_specs=(tokens, tokens, w_in, w_out),
        check_vma=False,
    )
```

```python
import math

import jax
import jax.numpy as jnp
from jax import lax
from jax.experimental import pallas as pl
from jax.experimental.pallas import tpu as pltpu
from jax.sharding import Mesh, PartitionSpec as P

GELU_SCALE = math.sqrt(2.0 / math.pi)
CUBIC = 0.044715
BACK_DIMS = (((1,), (1,)), ((), ()))
LEAD_DIMS = (((0,), (0,)), ((), ()))
PLAIN_DIMS = (((1,), (0,)), ((), ()))
AXES = ("b", "c", "x", "z", "a")
BF16, F32 = jnp.bfloat16, jnp.float32
ANY = pl.BlockSpec(memory_space=pl.ANY)
SMEM = pl.BlockSpec(memory_space=pltpu.SMEM)
WHOLE = pl.BlockSpec(memory_space=pltpu.VMEM)
SMALL = pl.CostEstimate(flops=1024, bytes_accessed=1024, transcendentals=0)


def place(x, y, z, c):
    b, a = divmod(y % 4, 2)
    return (((b * 2 + c) * 4 + x % 4) * 4 + z % 4) * 2 + a


def shift(value, dx=0, dy=0, dz=0, fc=0):
    pairs = [
        (place(x, y, z, c), place(x + dx, y + dy, z + dz, c ^ fc))
        for x in range(4)
        for y in range(4)
        for z in range(4)
        for c in range(2)
    ]
    return lax.ppermute(value, AXES, pairs)


def mul(left, right, dims):
    return lax.dot_general(left, right, dims, preferred_element_type=F32).astype(BF16)


def gelu_both(value):
    inner = GELU_SCALE * (value + CUBIC * value * value * value)
    tanh_value = jnp.tanh(inner)
    slope = 0.5 * (1.0 + tanh_value) + 0.5 * value * (1.0 - tanh_value * tanh_value) * GELU_SCALE * (
        1.0 + 3.0 * CUBIC * value * value
    )
    return 0.5 * value * (1.0 + tanh_value), slope


def at(blocks, index):
    return lax.dynamic_index_in_dim(blocks, index, 0, keepdims=False)


def after(value, *others):
    return lax.optimization_barrier((value,) + others)[0]


def call(kernel, name, outs, operands, specs=None, scratch=(), after=(), vmem=12, grid=(), out_specs=None):
    n, m = len(operands), len(after)

    def waiting(*refs):
        kernel(*refs[:n], *refs[n + m :])

    return pl.pallas_call(
        waiting,
        grid=grid,
        out_shape=[jax.ShapeDtypeStruct(shape, BF16) for shape in outs],
        in_specs=list(specs or [ANY] * n) + [ANY] * m,
        out_specs=out_specs or [WHOLE] * len(outs),
        scratch_shapes=list(scratch),
        compiler_params=pltpu.CompilerParams(vmem_limit_bytes=vmem * 1024 * 1024),
        cost_estimate=SMALL,
        name=name,
    )(*operands, *after)


def numbers_of(numbers):
    return jnp.stack([jnp.int32(number) for number in numbers])


def start(copies):
    for copy in copies:
        copy.start()
    return copies


def finish(copies):
    for copy in copies:
        copy.wait()


def spread(blocks, after):
    def kernel(*refs):
        outs, sems = refs[4:6], refs[6]
        finish(
            start(
                [
                    pltpu.make_async_copy(refs[i].at[pl.ds(h * 32, 32)], outs[h].at[pl.ds(i * 32, 32)], sems.at[i, h])
                    for i in range(4)
                    for h in range(2)
                ]
            )
        )

    return call(kernel, "spread", [(128, 1536)] * 2, blocks, None, [pltpu.SemaphoreType.DMA((4, 2))], after, 4)


def held(rows, after):
    def kernel(rows_ref, out_ref, sem):
        finish(start([pltpu.make_async_copy(rows_ref, out_ref, sem.at[0])]))

    return call(kernel, "held", [rows.shape], [rows], None, [pltpu.SemaphoreType.DMA((1,))], after, 4)[0]


def copied(shape, parts, after=()):
    n = len(parts)

    def kernel(numbers, *refs):
        out, sems = refs[n], refs[n + 1]
        copies = []
        for i in range(n):
            rows = refs[i].shape[0]
            col, row, out_col = (numbers[3 * i + k] for k in range(3))
            source = refs[i].at[:, pl.ds(pl.multiple_of(col * 1536, 1536), 1536)]
            target = out.at[pl.ds(pl.multiple_of(row * rows, rows), rows), pl.ds(pl.multiple_of(out_col * 1536, 1536), 1536)]
            copies.append(pltpu.make_async_copy(source, target, sems.at[i]))
        finish(start(copies))

    return call(
        kernel,
        "copied",
        [shape],
        [numbers_of([v for part in parts for v in part[1:]]), *[part[0] for part in parts]],
        [SMEM] + [ANY] * n,
        [pltpu.SemaphoreType.DMA((n,))],
        after,
        6,
    )[0]


def last(terms, after):
    def kernel(*refs):
        result = total([ref[...] for ref in refs[:4]]).astype(BF16)
        refs[4][...], refs[5][...] = result[:32], result[32:]

    return call(kernel, "last", [(32, 1536)] * 2, terms, [WHOLE] * 4, (), after, 4)


def put(parts, split=1):
    blocks = [block for _, block in parts]
    n, rows, width = len(parts), blocks[0].shape[0] // split, blocks[0].shape[1]

    def kernel(index_ref, *refs):
        outs, sems = refs[n : n + split], refs[n + split]
        copies = [
            pltpu.make_async_copy(
                refs[i].at[pl.ds(h * rows, rows)],
                outs[h].at[pl.ds(pl.multiple_of(index_ref[i] * rows, rows), rows)],
                sems.at[i, h],
            )
            for i in range(n)
            for h in range(split)
        ]
        for copy in copies:
            copy.start()
        for copy in copies:
            copy.wait()

    return pl.pallas_call(
        kernel,
        out_shape=[jax.ShapeDtypeStruct((n * rows, width), BF16)] * split,
        in_specs=[pl.BlockSpec(memory_space=pltpu.SMEM)] + [pl.BlockSpec(memory_space=pl.ANY)] * n,
        out_specs=[pl.BlockSpec(memory_space=pltpu.VMEM)] * split,
        scratch_shapes=[pltpu.SemaphoreType.DMA((n, split))],
        compiler_params=pltpu.CompilerParams(vmem_limit_bytes=10 * 1024 * 1024),
        name="put",
    )(jnp.stack([jnp.int32(index) for index, _ in parts]), *blocks)


def product(blocks, places, weight, dims, keep=False, joined=False, after=(), first=(0,) * 4):
    wide, back = 512, dims == BACK_DIMS
    n, m = len(blocks), len(after)
    n_out = 1 if joined else n
    rows = 512 // n_out

    def kernel(place_ref, *refs):
        w_ref, refs_after = refs[n], refs[n + 1 + m :]
        outs, rest = refs_after[:n_out], refs_after[n_out:]
        whole, sems = rest[0], rest[1]

        @pl.when(pl.program_id(0) == 0)
        def _():
            copies = [
                pltpu.make_async_copy(
                    refs[i].at[pl.ds(first[i], 128)],
                    whole.at[pl.ds(pl.multiple_of(place_ref[i] * 128, 128), 128)],
                    sems.at[i],
                )
                for i in range(n)
            ]
            for copy in copies:
                copy.start()
            for copy in copies:
                copy.wait()

        result = lax.dot_general(whole[...], w_ref[...], dims, preferred_element_type=F32).astype(BF16)
        for i in range(n_out):
            outs[i][...] = result[i * rows : (i + 1) * rows]

    w_block = ((wide, 1536), lambda t: (t, 0)) if back else ((1536, wide), lambda t: (0, t))
    out_shape = [jax.ShapeDtypeStruct((rows, 1536), BF16)] * n_out
    out_specs = [pl.BlockSpec((rows, wide), lambda t: (0, t))] * n_out
    scratch = [pltpu.VMEM((512, 1536), BF16), pltpu.SemaphoreType.DMA((n,))]
    if keep:
        out_shape.append(jax.ShapeDtypeStruct((512, 1536), BF16))
        out_specs.append(pl.BlockSpec((512, 1536), lambda t: (0, 0)))
        scratch = scratch[1:]
    return pl.pallas_call(
        kernel,
        grid=(1536 // wide,),
        out_shape=out_shape,
        in_specs=[pl.BlockSpec(memory_space=pltpu.SMEM)]
        + [pl.BlockSpec(memory_space=pl.ANY)] * n
        + [pl.BlockSpec(*w_block)]
        + [pl.BlockSpec(memory_space=pl.ANY)] * m,
        out_specs=out_specs,
        scratch_shapes=scratch,
        compiler_params=pltpu.CompilerParams(vmem_limit_bytes=16 * 1024 * 1024),
        cost_estimate=pl.CostEstimate(flops=2 * 512 * 1536 * 1536, bytes_accessed=8 << 20, transcendentals=0),
        name="product",
    )(jnp.stack([jnp.int32(place) for place in places]), *blocks, weight, *after)


def total(parts):
    result = parts[0].astype(F32)
    for part in parts[1:]:
        result = result + part.astype(F32)
    return result


def terms_of(rows, me, axis):
    blocks = rows.reshape(4, rows.shape[0] // 4, rows.shape[1])
    return [at(blocks, me)] + [shift(at(blocks, (me + i) % 4), **{axis: i}) for i in (1, 2, 3)]


def summed(rows, me, axis):
    return total(terms_of(rows, me, axis))


def scatter(parts, axis):
    return [parts[0]] + [shift(parts[i], **{axis: i}) for i in (1, 2, 3)]


def gather(block, axis):
    return [block] + [shift(block, **{axis: -i}) for i in (1, 2, 3)]


def body(inputs, in_weight, out_weight, out_grad):
    b, c, x, z = (lax.axis_index(name) for name in ("b", "c", "x", "z"))
    units = 1536
    quarters = (0, 128, 256, 384)
    in_z = [(x + i) % 4 for i in range(4)]
    to_x = [(z + i - x) % 4 for i in range(4)]
    to_z = [(x + i - z) % 4 for i in range(4)]

    out_other = shift(out_weight, fc=1)
    own = lax.dynamic_slice(in_weight, (0, b * units), (384, units))
    own_other = shift(own, fc=1)
    both = gather(jnp.concatenate([out_grad, inputs]), "dy")
    grad_128, tok_128 = spread(both, [out_other])
    grad_blocks = gather(grad_128, "dz")
    away = shift(after(lax.dynamic_slice(in_weight, (0, (1 - b) * units), (384, units)), grad_128), dy=2)

    (out_tile,) = put([(c, out_weight), (1 - c, out_other)])
    *grad_parts, grad_rows = product(grad_blocks, to_x, out_tile, BACK_DIMS, True)
    grad_act = total(scatter(grad_parts, "dx"))

    tok_rows = lax.all_gather(after(tok_128, *grad_blocks), "z", axis=0, tiled=True)
    away = after(away, grad_parts[0])
    (in_tile,) = put(
        [
            (2 * b + c, own),
            (2 * (1 - b) + c, away),
            (2 * b + 1 - c, own_other),
            (2 * (1 - b) + 1 - c, shift(away, fc=1)),
        ]
    )
    preact = summed(mul(tok_rows, in_tile, PLAIN_DIMS), x, "dx")
    act, slope = gelu_both(preact)
    pre_blocks = gather((grad_act * slope).astype(BF16), "dx")
    act_blocks = gather(after(act.astype(BF16), *pre_blocks), "dx")

    (grad_pre,) = put(list(zip(in_z, pre_blocks)))

    def columns(which):
        return jnp.concatenate(
            [lax.dynamic_slice(tok_rows, (0, (2 * i + which) * 384), (512, 384)) for i in range(2)], axis=1
        )

    tok_mine, tok_other = columns(c), columns(1 - c)

    other = shift(mul(tok_other, grad_pre, LEAD_DIMS), fc=1)
    in_part = mul(grad_pre, in_tile, BACK_DIMS)
    in_rows = lax.psum_scatter(in_part, "z", scatter_dimension=0, tiled=True)
    rows = total([mul(tok_mine, grad_pre, LEAD_DIMS), other]).astype(BF16).reshape(2, 384, units)
    kept, sent = at(rows, b), at(rows, 1 - b)
    arrived = shift(sent, dy=2)
    act_blocks[0] = after(act_blocks[0], sent)
    (act_rows,) = put(list(enumerate(act_blocks)))
    out_terms = terms_of(mul(act_rows, out_tile, PLAIN_DIMS), (z - x) % 4, "dz")
    grad_w_out = lax.psum_scatter(mul(act_rows, grad_rows, LEAD_DIMS), "c", scatter_dimension=0, tiled=True)
    out_terms[1], arrived = lax.optimization_barrier((out_terms[1], arrived))
    out_rows = total(out_terms).astype(BF16)
    grad_w_in = copied((384, 2 * units), [(kept, 0, 0, b), (arrived, 0, 0, 1 - b)])
    parts = [jnp.concatenate([v[i * 32 : (i + 1) * 32] for v in (out_rows, in_rows)]) for i in range(4)]
    return (*last(scatter(parts, "dy"), []), grad_w_in, grad_w_out)


def solution(mesh):
    fine = Mesh(mesh.devices.reshape(2, 2, 4, 4, 2), AXES)
    tokens = P(("b", "c", "z", "a"), "x")
    w_in = P(("x", "b", "c"), ("z", "a"))
    w_out = P(("z", "a", "b", "c"), "x")
    return jax.shard_map(
        body,
        mesh=fine,
        in_specs=(tokens, w_in, w_out, tokens),
        out_specs=(tokens, tokens, w_in, w_out),
        check_vma=False,
    )
```
